32 devices in a mesh: kvh: 2 (over y), qh: 4 (over x, core), req: 4 (over z).
Axes of the slice: x: 2, y: 2, z: 4, core: 2. Of those that a mesh axis runs over, the one named last changes fastest.
Arguments:
- queries: bfloat16 [8, 1024, 64, 128], P('req', None, ('kvh', 'qh')), may hold values from -12 to 12
- stretch_keys: bfloat16 [8, 1024, 8, 128], P('req', 'qh', 'kvh'), may hold values from -6 to 6
- stretch_values: bfloat16 [8, 1024, 8, 128], P('req', 'qh', 'kvh'), may hold values from -6 to 6
- cache_keys: bfloat16 [8, 1024, 8, 128], P('req', None, 'kvh'), may hold values from -6 to 6
- cache_values: bfloat16 [8, 1024, 8, 128], P('req', None, 'kvh'), may hold values from -6 to 6
- slot_of_req: int32 [8], replicated, may hold values from 0 to 7, each once
- cache_len: int32 [8], P('req'), may hold values from 128 to 1024, as said below
Outputs:
- attended: bfloat16 [8, 1024, 64, 128], P('req', None, ('kvh', 'qh'))
The draws below stay inside these ranges and needn't reach their ends.
Inputs may be any that keep to these rules, and one draw needn't show every extreme that they name: `cache_len`: one request in every draw has exactly 1024 cached positions.
All inputs are finite; a program needn't handle non-finite values.
Results may differ from the reference program's by a relative error of at most 0.0035.
Values may be sent and summed in bfloat16 or wider, within the bound.
No kernel may reach another device: no remote copies, remote signals or barrier semaphores. Data moves between devices by JAX's collectives and lax.ppermute only.
A program may use at most 64 MiB of HBM per device.

```python
import jax
import jax.numpy as jnp
from jax import lax

H = 64
KVH = 8
HD = 128
STRETCH = 1024
CACHE_LEN = 1024
REQS = 8


def draw_queries(key, part):
    shape = (REQS, STRETCH, H, HD)
    base = jnp.clip(2.0 * jax.random.normal(jax.random.fold_in(key, 1), shape, jnp.float32), -12.0, 12.0)
    return base.astype(jnp.bfloat16)


def draw_cache_keys(key, part):
    shape = (REQS, CACHE_LEN, KVH, HD)
    base = jnp.clip(jax.random.normal(jax.random.fold_in(key, 2), shape, jnp.float32), -6.0, 6.0)
    return base.astype(jnp.bfloat16)


def draw_cache_len(key, part):
    lengths = jax.random.randint(jax.random.fold_in(key, 11), (REQS,), CACHE_LEN // 8, CACHE_LEN + 1, dtype=jnp.int32)
    longest = jax.random.randint(jax.random.fold_in(key, 12), (), 0, REQS, dtype=jnp.int32)
    return jnp.where(jnp.arange(REQS, dtype=jnp.int32) == longest, CACHE_LEN, lengths).astype(jnp.int32)


def steps_of(own_key, extent, shards, smallest, largest):
    def one(dim, shards_of):
        steps = jax.random.uniform(jax.random.fold_in(jax.random.fold_in(own_key, 6), dim), (shards_of,), jnp.float32, smallest / len(shards), largest / len(shards))
        return jnp.repeat(jnp.exp(steps), extent[dim] // shards_of).reshape((-1,) + (1,) * (len(extent) - dim - 1))

    gain = one(*shards[0])
    for cut in shards[1:]:
        gain = gain * one(*cut)
    return gain


def scatter_about(own_key, extent, deviation, most, cuts=(), held_as=jnp.bfloat16):
    level = steps_of(own_key, extent, cuts, -0.22, 0.18) if cuts else 1.0
    array = jax.random.normal(own_key, extent, jnp.float32) * deviation * level
    return jnp.minimum(jnp.maximum(array, -most), most).astype(held_as)


def setup_inputs(seed: int = 0) -> dict:
    key_list = jax.random.split(jax.random.key(seed), 8)
    return {
        "queries": draw_queries(jax.random.fold_in(key_list[7], 71), 0),
        "stretch_keys": scatter_about(key_list[1], (REQS, STRETCH, KVH, HD), 1.0, 6.0, ((0, 4), (1, 4), (2, 2))),
        "stretch_values": scatter_about(key_list[2], (REQS, STRETCH, KVH, HD), 1.0, 6.0, ((0, 4), (1, 4), (2, 2))),
        "cache_keys": draw_cache_keys(jax.random.fold_in(key_list[7], 71), 0),
        "cache_values": scatter_about(key_list[4], (REQS, CACHE_LEN, KVH, HD), 1.0, 6.0, ((0, 4), (2, 2))),
        "slot_of_req": jax.random.permutation(key_list[5], REQS).astype(jnp.int32),
        "cache_len": draw_cache_len(jax.random.fold_in(key_list[7], 71), 0),
    }


def attend_request(inputs):
    query, keys_cache, values_cache, keys_stretch, values_stretch, length = inputs
    group = H // KVH
    factor = HD ** -0.5

    def per_group(index):
        query_part = lax.dynamic_slice_in_dim(query, index * group, group, 1).astype(jnp.float32)
        key_c = lax.dynamic_index_in_dim(keys_cache, index, 1, keepdims=False).astype(jnp.float32)
        value_c = lax.dynamic_index_in_dim(values_cache, index, 1, keepdims=False).astype(jnp.float32)
        key_n = lax.dynamic_index_in_dim(keys_stretch, index, 1, keepdims=False).astype(jnp.float32)
        value_n = lax.dynamic_index_in_dim(values_stretch, index, 1, keepdims=False).astype(jnp.float32)
        score_c = jnp.einsum("thd,pd->htp", query_part, key_c) * factor
        score_n = jnp.einsum("thd,ud->htu", query_part, key_n) * factor
        seen_c = (jnp.arange(CACHE_LEN, dtype=jnp.int32) < length)[None, None, :]
        seen_n = (jnp.arange(STRETCH, dtype=jnp.int32)[None, :] <= jnp.arange(STRETCH, dtype=jnp.int32)[:, None])[None]
        top_c = jnp.max(jnp.where(seen_c, score_c, -jnp.inf), axis=2)
        top_n = jnp.max(jnp.where(seen_n, score_n, -jnp.inf), axis=2)
        top = jnp.maximum(top_c, top_n)[:, :, None]
        weight_c = jnp.where(seen_c, jnp.exp(score_c - top), 0.0)
        weight_n = jnp.where(seen_n, jnp.exp(score_n - top), 0.0)
        total = jnp.sum(weight_c, axis=2) + jnp.sum(weight_n, axis=2)
        rounded_c = lax.optimization_barrier(weight_c.astype(jnp.bfloat16)).astype(jnp.float32)
        rounded_n = lax.optimization_barrier(weight_n.astype(jnp.bfloat16)).astype(jnp.float32)
        mixed = jnp.einsum("htp,pd->thd", rounded_c, value_c) + jnp.einsum("htu,ud->thd", rounded_n, value_n)
        return (mixed / jnp.transpose(total)[:, :, None]).astype(jnp.bfloat16)

    outputs = lax.map(per_group, jnp.arange(KVH, dtype=jnp.int32))
    return jnp.transpose(outputs, (1, 0, 2, 3)).reshape(STRETCH, H, HD)


def reference(queries, stretch_keys, stretch_values, cache_keys, cache_values, slot_of_req, cache_len):
    cached_keys = jnp.take(cache_keys, slot_of_req, axis=0)
    cached_values = jnp.take(cache_values, slot_of_req, axis=0)
    return lax.map(attend_request, (queries, cached_keys, cached_values, stretch_keys, stretch_values, cache_len))
```

```python
import functools
import itertools

import jax
import jax.numpy as jnp
from jax import lax
from jax.experimental import pallas as pl
from jax.experimental.pallas import tpu as pltpu
from jax.sharding import PartitionSpec as P

H = 64
KVH = 8
LOG2E = 1.4426950408889634
UNIT = 256
TILE = 1024
SURE = 128
ONES = 16
CEILING = 2.0**100


def dot(a, b, dims):
    return lax.dot_general(a, b, (dims, ((), ())), preferred_element_type=jnp.float32)


def attend_kernel(heads, which, lengths, q_ref, cache_ref, new_ref, _, out_ref, keys, flipped, total):
    span, depth = cache_ref.shape[1:]
    shares, _, _, share, _ = new_ref.shape
    block = q_ref.shape[1]
    tile = min(TILE, block)
    tiles = [slice(first, first + tile) for first in range(0, block, tile)]
    factor = depth**-0.5 * LOG2E
    index = pl.program_id(0)
    length = lengths[which[0]]
    cached = (length + UNIT - 1) // UNIT
    count = cached + index

    @pl.when(index == 0)
    def prepare():
        seen = lax.broadcasted_iota(jnp.int32, (span, depth), 0) < length
        keys[:span] = jnp.where(seen, cache_ref[0], cache_ref[0, 0:1])
        values = jnp.where(seen, cache_ref[1], jnp.zeros_like(cache_ref[1])).astype(jnp.float32)
        flipped[:depth, :span] = values.T.astype(jnp.bfloat16)
        column = lax.broadcasted_iota(jnp.int32, (ONES, span), 1)
        flipped[depth:, :span] = jnp.where(column < length, 1.0, 0.0).astype(jnp.bfloat16)
        for n in range(shares):
            at = pl.ds(pl.multiple_of(cached * UNIT + n * share, 128), share)
            keys[at] = new_ref[n, 0, 0]
            flipped[:depth, at] = new_ref[n, 1, 0].astype(jnp.float32).T.astype(jnp.bfloat16)
            flipped[depth:, at] = jnp.ones((ONES, share), jnp.bfloat16)

    def score(at, cut, size):
        return dot(keys[pl.ds(at, size)], q_ref[0, cut], ((1,), (1,)))

    def mix(at, weights, size):
        return dot(flipped[:, pl.ds(at, size)], weights.astype(jnp.bfloat16), ((1,), (0,)))

    top = jnp.max(dot(keys[:SURE], q_ref[0], ((1,), (1,))), axis=0, keepdims=True) * factor
    total[...] = jnp.zeros_like(total)

    def step(pair, carry):
        at = pl.multiple_of(pair * 2 * UNIT, 2 * UNIT)
        scores = score(at, tiles[0], 2 * UNIT)
        for n, cut in enumerate(tiles):
            later = score(at, tiles[n + 1], 2 * UNIT) if n + 1 < len(tiles) else None
            total[:, cut] += mix(at, jnp.exp2(scores * factor - top[:, cut]), 2 * UNIT)
            scores = later
        return carry

    lax.fori_loop(0, count // 2, step, 0)

    def finish(lone):
        at = pl.multiple_of((count - lone) * UNIT, UNIT)
        sizes = [lone * UNIT + (n + 1) * tile // heads for n in range(len(tiles))]
        scores = score(at, tiles[0], sizes[0])
        for n, cut in enumerate(tiles):
            later = score(at, tiles[n + 1], sizes[n + 1]) if n + 1 < len(tiles) else None
            weights = jnp.exp2(scores * factor - top[:, cut])
            key = lax.broadcasted_iota(jnp.int32, scores.shape, 0) - lone * UNIT
            token = (lax.broadcasted_iota(jnp.int32, scores.shape, 1) + n * tile) // heads
            mixed = total[:, cut] + mix(at, jnp.where(key <= token, weights, 0.0), sizes[n])
            total[:, cut] = mixed
            out_ref[0, cut] = (mixed[:depth] / mixed[depth : depth + 1]).T.astype(jnp.bfloat16)
            scores = later

    pl.when(count % 2 == 1)(functools.partial(finish, 1))
    pl.when(count % 2 == 0)(functools.partial(finish, 0))

    @pl.when(jnp.logical_not(jnp.max(total[depth : depth + 1]) < CEILING))
    def redo():
        small = UNIT

        def column(c, carry):
            cut = pl.ds(pl.multiple_of(c * small, small), small)
            query = q_ref[0, cut]

            def unit(u, state):
                highest, mixed = state
                at = pl.multiple_of(u * UNIT, UNIT)
                scores = dot(keys[pl.ds(at, UNIT)], query, ((1,), (1,))) * factor
                key = lax.broadcasted_iota(jnp.int32, scores.shape, 0)
                token = (lax.broadcasted_iota(jnp.int32, scores.shape, 1) + c * small) // heads
                scores = jnp.where((key <= token) | (u < count), scores, -jnp.inf)
                higher = jnp.maximum(highest, jnp.max(scores, axis=0, keepdims=True))
                weights = jnp.exp2(scores - higher)
                return higher, mixed * jnp.exp2(highest - higher) + mix(at, weights, UNIT)

            first = (jnp.full((1, small), -1e30, jnp.float32), jnp.zeros((depth + ONES, small), jnp.float32))
            _, mixed = lax.fori_loop(0, count + 1, unit, first)
            out_ref[0, cut] = (mixed[:depth] / mixed[depth : depth + 1]).T.astype(jnp.bfloat16)
            return carry

        lax.fori_loop(0, block // small, column, 0)


def attend(heads, which, lengths, queries, cache, new, before=None):
    requests, rows, depth = queries.shape
    shares, _, _, share, _ = new.shape
    span = cache.shape[1]
    block = UNIT * heads
    if before is None:
        before = jnp.zeros((8, depth), jnp.bfloat16)
        alias = {}
    else:
        alias = {5: 0}
    return pl.pallas_call(
        functools.partial(attend_kernel, heads),
        grid_spec=pltpu.PrefetchScalarGridSpec(
            num_scalar_prefetch=2,
            grid=(rows // block,),
            in_specs=[
                pl.BlockSpec((1, block, depth), lambda i, which, _: (which[0], i, 0)),
                pl.BlockSpec((2, span, depth), lambda i, *_: (0, 0, 0)),
                pl.BlockSpec((shares, 2, 1, share, depth), lambda i, which, _: (0, 0, which[0], 0, 0)),
                pl.BlockSpec(memory_space=pl.ANY),
            ],
            out_specs=pl.BlockSpec((1, block, depth), lambda i, which, _: (which[0], i, 0)),
            scratch_shapes=[
                pltpu.VMEM((span + shares * share, depth), jnp.bfloat16),
                pltpu.VMEM((depth + ONES, span + shares * share), jnp.bfloat16),
                pltpu.VMEM((depth + ONES, block), jnp.float32),
            ],
        ),
        out_shape=jax.ShapeDtypeStruct(queries.shape, jnp.bfloat16),
        input_output_aliases=alias,
        compiler_params=pltpu.CompilerParams(vmem_limit_bytes=60 << 20),
        name="attend",
    )(which, lengths, queries, cache, new, before)


def one_head(array, head):
    return lax.dynamic_index_in_dim(array, head, 2, keepdims=False)


def exchange_stretch(keys, values, per_device, group):
    devices = lax.axis_size("qh")
    parts = [jnp.stack([a[:, :, n * per_device // group] for a in (keys, values)]) for n in range(devices)]
    return lax.all_to_all(jnp.stack(parts), "qh", split_axis=0, concat_axis=0, tiled=True)


def plan_rounds(slot_of_req):
    source = slot_of_req // 2
    choices = jnp.array(list(itertools.product(range(2), repeat=4)), jnp.int32)
    first = jnp.where(choices == 0, source[0::2], source[1::2])
    second = jnp.where(choices == 0, source[1::2], source[0::2])
    target = jnp.arange(4, dtype=jnp.int32)

    def load(origin):
        right = [jnp.sum((origin <= n) & (target > n), axis=1) for n in range(3)]
        left = [jnp.sum((origin > n) & (target <= n), axis=1) for n in range(3)]
        return functools.reduce(jnp.maximum, right + left)

    fits = jnp.sum(1 << first, axis=1) == 15
    cost = jnp.where(fits, load(first) + load(second), 100)
    best = jnp.argmin(cost).astype(jnp.int32)
    chosen = (jnp.arange(16) == best)[:, None]
    order = jnp.array(list(itertools.permutations(range(4))), jnp.int32)
    rounds = []
    for flip, origin in ((0, first), (1, second)):
        picked = jnp.sum(jnp.where(chosen, choices ^ flip, 0), axis=0)
        origin = jnp.sum(jnp.where(chosen, origin, 0), axis=0)
        place = jnp.argmax(jnp.all(order == origin, axis=1)).astype(jnp.int32)
        rounds.append((picked, place))
    return rounds


def on_device(queries, stretch_keys, stretch_values, cache_keys, cache_values, slot_of_req, cache_len):
    req_count = lax.axis_size("req")
    local_reqs, stretch, head_count, depth = queries.shape
    group = H // KVH
    kv_local = lax.axis_index("qh") * head_count // group
    new = exchange_stretch(stretch_keys, stretch_values, head_count, group)
    held = jnp.stack([one_head(cache_keys, kv_local), one_head(cache_values, kv_local)], axis=1)
    flat = queries.reshape(local_reqs, stretch * head_count, depth)
    out = None
    if req_count == 4 and local_reqs == 2:
        me = lax.axis_index("req")
        slots = slot_of_req.reshape(4, 2)
        for picked, place in plan_rounds(slot_of_req):
            slot = jnp.where(picked == 0, slots[:, 0], slots[:, 1])
            sent = jnp.sum(jnp.where(slot // 2 == me, slot % 2, 0))
            block = lax.dynamic_index_in_dim(held, sent, 0, keepdims=False)
            routes = [
                functools.partial(lambda pairs, a: lax.ppermute(a, "req", pairs), [(s, d) for d, s in enumerate(p)])
                for p in itertools.permutations(range(4))
            ]
            cache = lax.switch(place, routes, block)
            which = lax.dynamic_index_in_dim(picked, me, 0)
            out = attend(head_count, which, cache_len, flat, cache, new, out)
    else:
        caches = relocate(held, slot_of_req, req_count)
        for n in range(local_reqs):
            out = attend(head_count, jnp.array([n], jnp.int32), cache_len, flat, caches[n], new, out)
    return out.reshape(queries.shape)


def relocate(held, slot_of_req, req_count):
    slots, two, span, depth = held.shape
    split = held.reshape(slots, two, req_count, span // req_count, depth)
    spread = lax.all_to_all(split, "req", split_axis=2, concat_axis=0, tiled=True)
    picked = jnp.take(spread, slot_of_req, axis=0)
    got = lax.all_to_all(picked, "req", split_axis=0, concat_axis=2, tiled=True)
    return got.reshape(slots, two, span, depth)


def solution(mesh):
    return jax.shard_map(
        on_device,
        mesh=mesh,
        in_specs=(
            P("req", None, ("kvh", "qh"), None),
            P("req", "qh", "kvh", None),
            P("req", "qh", "kvh", None),
            P("req", None, "kvh", None),
            P("req", None, "kvh", None),
            P(),
            P("req"),
        ),
        out_specs=P("req", None, ("kvh", "qh"), None),
        check_vma=False,
    )
```

```python
import functools
import itertools

import jax
import jax.numpy as jnp
from jax import lax
from jax.experimental import pallas as pl
from jax.experimental.pallas import tpu as pltpu
from jax.sharding import PartitionSpec as P

H = 64
KVH = 8
LOG2E = 1.4426950408889634
UNIT = 256
TOKENS = 1024
TILE = 1024
SURE = 128
ONES = 16
CEILING = 2.0**100


def dot(a, b, dims):
    return lax.dot_general(a, b, (dims, ((), ())), preferred_element_type=jnp.float32)


def attend_kernel(heads, which, lengths, q_ref, *refs):
    *cache_refs, new_ref, out_ref, keys, flipped, total, top = refs
    span, depth = cache_refs[0].shape[1:]
    shares, _, _, share, _ = new_ref.shape
    block = q_ref.shape[1]
    tile = min(TILE, block)
    tiles = [slice(first, first + tile) for first in range(0, block, tile)]
    units = block // heads // UNIT
    factor = depth**-0.5 * LOG2E
    order = pl.program_id(0)
    index = pl.program_id(1)
    request = which[order]
    length = lengths[request]
    cached = (length + UNIT - 1) // UNIT
    count = cached + index * units

    def prepare(cache_ref):
        seen = lax.broadcasted_iota(jnp.int32, (span, depth), 0) < length
        keys[:span] = jnp.where(seen, cache_ref[0], cache_ref[0, 0:1])
        values = jnp.where(seen, cache_ref[1], jnp.zeros_like(cache_ref[1])).astype(jnp.float32)
        flipped[:depth, :span] = values.T.astype(jnp.bfloat16)
        column = lax.broadcasted_iota(jnp.int32, (ONES, span), 1)
        flipped[depth:, :span] = jnp.where(column < length, 1.0, 0.0).astype(jnp.bfloat16)
        for n in range(shares):
            at = pl.ds(pl.multiple_of(cached * UNIT + n * share, 128), share)
            keys[at] = new_ref[n, 0, request]
            flipped[:depth, at] = new_ref[n, 1, request].astype(jnp.float32).T.astype(jnp.bfloat16)
            flipped[depth:, at] = jnp.ones((ONES, share), jnp.bfloat16)

    for n, cache_ref in enumerate(cache_refs):
        pl.when((order == n) & (index == 0))(functools.partial(prepare, cache_ref))

    def score(at, cut, size):
        return dot(keys[pl.ds(at, size)], q_ref[0, cut], ((1,), (1,))) * factor

    def mix(at, weights, size):
        return dot(flipped[:, pl.ds(at, size)], weights.astype(jnp.bfloat16), ((1,), (0,)))

    def reference(scores, cut, first):
        mine = jnp.max(scores[:SURE], axis=0, keepdims=True)
        mine = jnp.where(first, mine, top[:, cut])
        top[:, cut] = mine
        return mine

    total[...] = jnp.zeros_like(total)

    def step(pair, carry):
        at = pl.multiple_of(pair * 2 * UNIT, 2 * UNIT)
        scores = score(at, tiles[0], 2 * UNIT)
        for n, cut in enumerate(tiles):
            later = score(at, tiles[n + 1], 2 * UNIT) if n + 1 < len(tiles) else None
            weights = jnp.exp2(scores - reference(scores, cut, pair == 0))
            total[:, cut] += mix(at, weights, 2 * UNIT)
            scores = later
        return carry

    lax.fori_loop(0, count // 2, step, 0)

    def finish(lone):
        at = pl.multiple_of((count - lone) * UNIT, UNIT)
        sizes = [lone * UNIT + (n + 1) * tile // heads for n in range(len(tiles))]
        scores = score(at, tiles[0], sizes[0])
        for n, cut in enumerate(tiles):
            later = score(at, tiles[n + 1], sizes[n + 1]) if n + 1 < len(tiles) else None
            base = reference(scores, cut, count < 2) if lone else top[:, cut]
            weights = jnp.exp2(scores - base)
            key = lax.broadcasted_iota(jnp.int32, scores.shape, 0) - lone * UNIT
            token = (lax.broadcasted_iota(jnp.int32, scores.shape, 1) + n * tile) // heads
            mixed = total[:, cut] + mix(at, jnp.where(key <= token, weights, 0.0), sizes[n])
            total[depth:, cut] = mixed[depth:]
            out_ref[0, cut] = (mixed[:depth] / mixed[depth : depth + 1]).T.astype(jnp.bfloat16)
            scores = later

    pl.when(count % 2 == 1)(functools.partial(finish, 1))
    pl.when(count % 2 == 0)(functools.partial(finish, 0))

    @pl.when(jnp.logical_not(jnp.max(total[depth : depth + 1]) < CEILING))
    def redo():
        small = UNIT

        def column(c, carry):
            cut = pl.ds(pl.multiple_of(c * small, small), small)
            query = q_ref[0, cut]

            def unit(u, state):
                highest, mixed = state
                at = pl.multiple_of(u * UNIT, UNIT)
                scores = dot(keys[pl.ds(at, UNIT)], query, ((1,), (1,))) * factor
                key = lax.broadcasted_iota(jnp.int32, scores.shape, 0) + (u - count) * UNIT
                token = (lax.broadcasted_iota(jnp.int32, scores.shape, 1) + c * small) // heads
                scores = jnp.where(key <= token, scores, -jnp.inf)
                higher = jnp.maximum(highest, jnp.max(scores, axis=0, keepdims=True))
                weights = jnp.exp2(scores - higher)
                return higher, mixed * jnp.exp2(highest - higher) + mix(at, weights, UNIT)

            first = (jnp.full((1, small), -1e30, jnp.float32), jnp.zeros((depth + ONES, small), jnp.float32))
            _, mixed = lax.fori_loop(0, count + units, unit, first)
            out_ref[0, cut] = (mixed[:depth] / mixed[depth : depth + 1]).T.astype(jnp.bfloat16)
            return carry

        lax.fori_loop(0, block // small, column, 0)


def attend(heads, which, lengths, queries, caches, new):
    requests, rows, depth = queries.shape
    shares, _, _, share, _ = new.shape
    span = caches[0].shape[1]
    block = TOKENS * heads
    part = pl.BlockSpec((1, block, depth), lambda n, i, which, _: (which[n], i, 0))
    whole = [pl.BlockSpec(a.shape, functools.partial(lambda rank, *_: (0,) * rank, a.ndim)) for a in (*caches, new)]
    return pl.pallas_call(
        functools.partial(attend_kernel, heads),
        grid_spec=pltpu.PrefetchScalarGridSpec(
            num_scalar_prefetch=2,
            grid=(requests, rows // block),
            in_specs=[part, *whole],
            out_specs=part,
            scratch_shapes=[
                pltpu.VMEM((span + shares * share, depth), jnp.bfloat16),
                pltpu.VMEM((depth + ONES, span + shares * share), jnp.bfloat16),
                pltpu.VMEM((depth + ONES, block), jnp.float32),
                pltpu.VMEM((1, block), jnp.float32),
            ],
        ),
        out_shape=jax.ShapeDtypeStruct(queries.shape, jnp.bfloat16),
        compiler_params=pltpu.CompilerParams(vmem_limit_bytes=60 << 20),
        name="attend",
    )(which, lengths, queries, *caches, new)


def pick_rows(ref, picks, heads, depth):
    chunk = 256
    positions = chunk // heads
    kept = len(picks) * positions
    row = lax.broadcasted_iota(jnp.int32, (kept, chunk), 0)
    column = lax.broadcasted_iota(jnp.int32, (kept, chunk), 1)
    wanted = row % positions * heads
    for n, pick in enumerate(picks):
        wanted = wanted + jnp.where(row // positions == n, pick, 0)
    chosen = jnp.where(column == wanted, 1.0, 0.0).astype(jnp.bfloat16)
    parts = []
    for first in range(0, ref.shape[0], chunk):
        parts.append(dot(chosen, ref[first : first + chunk], ((1,), (0,))).astype(jnp.bfloat16))
    return [jnp.concatenate([p[n * positions : (n + 1) * positions] for p in parts]) for n in range(len(picks))]


def split_kernel(heads, picks, keys_ref, values_ref, out_ref):
    for kind, ref in enumerate((keys_ref, values_ref)):
        for n in range(ref.shape[0]):
            for place, rows in enumerate(pick_rows(ref.at[n], picks, heads, ref.shape[2])):
                out_ref[place, kind, n] = rows


def split_heads(keys, values, picks):
    requests, share, heads, depth = keys.shape
    rows = share * heads
    return pl.pallas_call(
        functools.partial(split_kernel, heads, picks),
        out_shape=jax.ShapeDtypeStruct((len(picks), 2, requests, share, depth), keys.dtype),
        name="split_heads",
    )(keys.reshape(requests, rows, depth), values.reshape(requests, rows, depth))


def take_kernel(heads, per_device, plan, keys_ref, values_ref, out_ref):
    head = lax.axis_index("qh") * per_device // (H // KVH)
    for kind, ref in enumerate((keys_ref, values_ref)):
        (out_ref[kind],) = pick_rows(ref.at[0], [head], heads, ref.shape[2])


def take_slot(keys, values, plan, entry, per_device):
    slots, span, heads, depth = keys.shape
    rows = span * heads
    steps = 2
    part = pl.BlockSpec((1, rows // steps, depth), lambda i, plan: (plan[entry], i, 0))
    return pl.pallas_call(
        functools.partial(take_kernel, heads, per_device),
        grid_spec=pltpu.PrefetchScalarGridSpec(
            num_scalar_prefetch=1,
            grid=(steps,),
            in_specs=[part, part],
            out_specs=pl.BlockSpec((2, span // steps, depth), lambda i, _: (0, i, 0)),
        ),
        out_shape=jax.ShapeDtypeStruct((2, span, depth), keys.dtype),
        name="take_slot",
    )(plan, keys.reshape(slots, rows, depth), values.reshape(slots, rows, depth))


def plan_kernel(slots, out):
    me = lax.axis_index("req")
    slot = [slots[n] for n in range(8)]
    source = [s // 2 for s in slot]

    def load(origin):
        flows = []
        for n in range(3):
            flows.append(sum((origin[d] <= n).astype(jnp.int32) for d in range(n + 1, 4)))
            flows.append(sum((origin[d] > n).astype(jnp.int32) for d in range(n + 1)))
        return functools.reduce(jnp.maximum, flows)

    least, best = jnp.int32(1000), jnp.int32(0)
    for choice in range(16):
        bits = [choice >> d & 1 for d in range(4)]
        first = [source[2 * d + bits[d]] for d in range(4)]
        second = [source[2 * d + 1 - bits[d]] for d in range(4)]
        met = sum(1 << s for s in first)
        cost = jnp.where(met == 15, 3 * load(first) + 2 * load(second), 999)
        best = jnp.where(cost < least, choice, best)
        least = jnp.minimum(cost, least)
    for n in range(2):
        bits = [(best >> d & 1) ^ n for d in range(4)]
        chosen = [jnp.where(bits[d] == 1, slot[2 * d + 1], slot[2 * d]) for d in range(4)]
        p = [s // 2 for s in chosen]
        out[n] = sum(jnp.where(me == d, bits[d], 0) for d in range(4))
        out[2 + n] = sum(jnp.where(p[d] == me, chosen[d] % 2, 0) for d in range(4))
        out[4 + n] = p[0] * 6 + (p[1] - (p[0] < p[1])) * 2 + (p[2] > p[3])


def plan_rounds(slot_of_req):
    smem = pl.BlockSpec(memory_space=pltpu.SMEM)
    return pl.pallas_call(
        plan_kernel,
        out_shape=jax.ShapeDtypeStruct((6,), jnp.int32),
        in_specs=[smem],
        out_specs=smem,
        name="plan_rounds",
    )(slot_of_req)


def routed(place, work):
    def branch(origins):
        pairs = [(s, d) for d, s in enumerate(origins)]
        return lambda *args: work(functools.partial(lax.ppermute, axis_name="req", perm=pairs), *args)

    return lambda *args: lax.switch(place, [branch(p) for p in itertools.permutations(range(4))], *args)


def on_device(queries, stretch_keys, stretch_values, cache_keys, cache_values, slot_of_req, cache_len):
    local_reqs, stretch, head_count, depth = queries.shape
    req_count = lax.axis_size("req")
    picks = [n * head_count // (H // KVH) for n in range(lax.axis_size("qh"))]
    flat = queries.reshape(local_reqs, stretch * head_count, depth)

    def exchange(blocks):
        return lax.all_to_all(blocks, "qh", split_axis=0, concat_axis=0, tiled=True)

    if req_count == 4 and local_reqs == 2:
        plan = plan_rounds(slot_of_req)

        def first_round(send, block, plan, keys, values, new_keys, new_values):
            later = take_slot(keys, values, plan, 3, head_count)
            return send(block), later, split_heads(new_keys, new_values, picks)

        block = take_slot(cache_keys, cache_values, plan, 2, head_count)
        first, block, blocks = routed(plan[4], first_round)(
            block, plan, cache_keys, cache_values, stretch_keys, stretch_values
        )
        new = exchange(blocks)
        second = routed(plan[5], lambda send, block: send(block))(block)
        caches = [first, second]
    else:
        new = exchange(split_heads(stretch_keys, stretch_values, picks))
        plan = jnp.arange(local_reqs, dtype=jnp.int32)
        held = [take_slot(cache_keys, cache_values, plan, n, head_count) for n in range(local_reqs)]
        held = relocate(jnp.stack(held), slot_of_req, req_count)
        caches = [held[n] for n in range(local_reqs)]
    out = attend(head_count, plan, cache_len, flat, caches, new)
    return out.reshape(queries.shape)


def relocate(held, slot_of_req, req_count):
    slots, two, span, depth = held.shape
    split = held.reshape(slots, two, req_count, span // req_count, depth)
    spread = lax.all_to_all(split, "req", split_axis=2, concat_axis=0, tiled=True)
    picked = jnp.take(spread, slot_of_req, axis=0)
    got = lax.all_to_all(picked, "req", split_axis=0, concat_axis=2, tiled=True)
    return got.reshape(slots, two, span, depth)


def solution(mesh):
    return jax.shard_map(
        on_device,
        mesh=mesh,
        in_specs=(
            P("req", None, ("kvh", "qh"), None),
            P("req", "qh", "kvh", None),
            P("req", "qh", "kvh", None),
            P("req", None, "kvh", None),
            P("req", None, "kvh", None),
            P(),
            P("req"),
        ),
        out_specs=P("req", None, ("kvh", "qh"), None),
        check_vma=False,
    )
```

```python
import functools

import jax
import jax.numpy as jnp
from jax import lax
from jax.experimental import pallas as pl
from jax.experimental.pallas import tpu as pltpu
from jax.sharding import PartitionSpec as P

H = 64
KVH = 8
LOG2E = 1.4426950408889634
UNIT = 256
TOKENS = 512
TILE = 1024
ONES = 16
CEILING = 2.0**100


def dot(a, b, dims):
    return lax.dot_general(a, b, (dims, ((), ())), preferred_element_type=jnp.float32)


def cut_tiles(block):
    tile = min(TILE, block)
    return tile, [slice(first, first + tile) for first in range(0, block, tile)]


def pick_rows(rows, picks, heads):
    chunk = min(256, rows.shape[0])
    positions = chunk // heads
    kept = len(picks) * positions
    row = lax.broadcasted_iota(jnp.int32, (kept, chunk), 0)
    column = lax.broadcasted_iota(jnp.int32, (kept, chunk), 1)
    wanted = row % positions * heads
    for n, pick in enumerate(picks):
        wanted = wanted + jnp.where(row // positions == n, pick, 0)
    chosen = jnp.where(column == wanted, 1.0, 0.0).astype(jnp.bfloat16)
    parts = []
    for first in range(0, rows.shape[0], chunk):
        parts.append(dot(chosen, rows[first : first + chunk], ((1,), (0,))).astype(jnp.bfloat16))
    return [jnp.concatenate([p[n * positions : (n + 1) * positions] for p in parts]) for n in range(len(picks))]


def ahead(n, devices, axis):
    return lax.rem(lax.axis_index(axis) + n, devices)


def send_back(blocks, axis):
    devices = len(blocks)
    pairs = [[(d, (d - n) % devices) for d in range(devices)] for n in range(devices)]
    return [blocks[0], *[lax.ppermute(blocks[n], axis, pairs[n]) for n in range(1, devices)]]


def split_kernel(heads, per_device, keys_ref, values_ref, _, *out_refs):
    devices = len(out_refs)
    picks = [ahead(devices - n, devices, "qh") * per_device // (H // KVH) for n in range(devices)]
    for kind, ref in enumerate((keys_ref, values_ref)):
        for n in range(ref.shape[0]):
            for out_ref, rows in zip(out_refs, pick_rows(ref.at[n], picks, heads)):
                out_ref[kind, n] = rows


def split_stretch(keys, values, per_device, after):
    requests, share, heads, depth = keys.shape
    rows = share * heads
    whole = pl.BlockSpec(memory_space=pltpu.VMEM)
    return pl.pallas_call(
        functools.partial(split_kernel, heads, per_device),
        in_specs=[whole, whole, pl.BlockSpec(memory_space=pl.ANY)],
        out_shape=[jax.ShapeDtypeStruct((2, requests, share, depth), keys.dtype)] * lax.axis_size("qh"),
        name="split_stretch",
    )(keys.reshape(requests, rows, depth), values.reshape(requests, rows, depth), after)


def share_kernel(heads, per_device, keys_ref, values_ref, *out_refs):
    head = lax.axis_index("qh") * per_device // (H // KVH)
    shares = len(out_refs)
    size = keys_ref.shape[1] // shares
    for n, out_ref in enumerate(out_refs):
        at = pl.ds(pl.multiple_of(ahead(shares - n, shares, "req") * size, size), size)
        for kind, ref in enumerate((keys_ref, values_ref)):
            for slot in range(ref.shape[0]):
                (out_ref[slot, kind],) = pick_rows(ref.at[slot, at], [head], heads)


def share_slots(keys, values, per_device):
    slots, span, heads, depth = keys.shape
    shares = lax.axis_size("req")
    block = jax.ShapeDtypeStruct((slots, 2, span // shares, depth), keys.dtype)
    return pl.pallas_call(
        functools.partial(share_kernel, heads, per_device),
        out_shape=[block] * shares,
        compiler_params=pltpu.CompilerParams(vmem_limit_bytes=30 << 20),
        name="share_slots",
    )(keys.reshape(slots, span * heads, depth), values.reshape(slots, span * heads, depth))


def order_kernel(local, slot_ref, *refs):
    shares = (len(refs) - 1) // (local + 1)
    spread_refs, out_refs = refs[:shares], refs[shares + 1 :]
    me = lax.axis_index("req")

    def take(out_ref, spread_ref, place):
        out_ref[...] = spread_ref[place]

    for n, out_ref in enumerate(out_refs):
        place, back = divmod(n, shares)
        slot = slot_ref[ahead(shares - back, shares, "req") * local + place]
        entry = lax.rem(slot // local + shares - me, shares)
        for m, spread_ref in enumerate(spread_refs):
            pl.when(entry == m)(functools.partial(take, out_ref, spread_ref, lax.rem(slot, local)))


def order_shares(spread, slot_of_req, after):
    shares, (local, two, share, depth) = len(spread), spread[0].shape
    whole = pl.BlockSpec(memory_space=pltpu.VMEM)
    blocks = pl.pallas_call(
        functools.partial(order_kernel, local),
        in_specs=[pl.BlockSpec(memory_space=pltpu.SMEM), *[whole] * shares, pl.BlockSpec(memory_space=pl.ANY)],
        out_shape=[jax.ShapeDtypeStruct((two, share, depth), spread[0].dtype)] * (local * shares),
        name="order_shares",
    )(slot_of_req, *spread, after)
    return [blocks[n * shares : (n + 1) * shares] for n in range(local)]


def stretch_kernel(heads, q_ref, *refs):
    *new_refs, _, state_ref, top_ref, keys, flipped = refs
    shares, (_, _, share, depth) = len(new_refs), new_refs[0].shape
    block = q_ref.shape[1]
    tile, tiles = cut_tiles(block)
    own = tile // heads
    factor = depth**-0.5 * LOG2E
    index = pl.program_id(0)

    @pl.when(index == 0)
    def prepare():
        for n, new_ref in enumerate(new_refs):
            at = pl.ds(pl.multiple_of(ahead(n, shares, "qh") * share, share), share)
            keys[at] = new_ref[0, 0]
            flipped[:depth, at] = new_ref[1, 0].astype(jnp.float32).T.astype(jnp.bfloat16)
        flipped[depth:] = jnp.ones((ONES, shares * share), jnp.bfloat16)

    def score(at, cut):
        return dot(keys[at], q_ref[0, cut], ((1,), (1,))) * factor

    def mix(at, weights):
        return dot(flipped[:, at], weights.astype(jnp.bfloat16), ((1,), (0,)))

    first = pl.multiple_of(index * (block // heads), block // heads)
    spans = [pl.ds(first, (n + 1) * own) for n in range(len(tiles))]
    key = lax.broadcasted_iota(jnp.int32, (own, tile), 0)
    token = lax.broadcasted_iota(jnp.int32, (own, tile), 1) // heads
    scores = score(spans[0], tiles[0])
    for n, cut in enumerate(tiles):
        later = score(spans[n + 1], tiles[n + 1]) if n + 1 < len(tiles) else None
        last = jnp.where(key <= token, scores[n * own :], -jnp.inf)
        base = jnp.max(last, axis=0, keepdims=True)
        top_ref[0, :, cut] = base
        weights = jnp.exp2(last - base)
        if n:
            weights = jnp.concatenate([jnp.exp2(scores[: n * own] - base), weights])
        state_ref[0, :, cut] = mix(spans[n], weights)
        scores = later

    def step(pair, carry):
        at = pl.ds(pl.multiple_of(pair * 2 * UNIT, 2 * UNIT), 2 * UNIT)
        scores = score(at, tiles[0])
        for n, cut in enumerate(tiles):
            later = score(at, tiles[n + 1]) if n + 1 < len(tiles) else None
            state_ref[0, :, cut] += mix(at, jnp.exp2(scores - top_ref[0, :, cut]))
            scores = later
        return carry

    lax.fori_loop(0, first // (2 * UNIT), step, 0)


def attend_stretch(heads, request, queries, new, after):
    _, rows, depth = queries.shape
    shares, share = len(new), new[0].shape[2]
    block = TOKENS * heads
    state = depth + ONES
    return pl.pallas_call(
        functools.partial(stretch_kernel, heads),
        grid=(rows // block,),
        in_specs=[
            pl.BlockSpec((1, block, depth), lambda i: (request, i, 0)),
            *[pl.BlockSpec((2, 1, share, depth), lambda i: (0, request, 0, 0))] * shares,
            pl.BlockSpec(memory_space=pl.ANY),
        ],
        out_specs=[
            pl.BlockSpec((1, state, block), lambda i: (0, 0, i)),
            pl.BlockSpec((1, 1, block), lambda i: (0, 0, i)),
        ],
        out_shape=[
            jax.ShapeDtypeStruct((1, state, rows), jnp.float32),
            jax.ShapeDtypeStruct((1, 1, rows), jnp.float32),
        ],
        scratch_shapes=[
            pltpu.VMEM((shares * share, depth), jnp.bfloat16),
            pltpu.VMEM((state, shares * share), jnp.bfloat16),
        ],
        compiler_params=pltpu.CompilerParams(vmem_limit_bytes=30 << 20),
        name="attend_stretch",
    )(queries, *new, after)


def cache_kernel(heads, request, shares, fresh, lengths, q_ref, state_ref, top_ref, *refs):
    cache_refs, new_refs = refs[:shares], refs[shares : shares + fresh]
    out_ref, keys, values, flipped, total = refs[-5:]
    _, share, depth = cache_refs[0].shape
    block = q_ref.shape[1]
    tile, tiles = cut_tiles(block)
    factor = depth**-0.5 * LOG2E
    index = pl.program_id(0)
    length = lengths[request]
    count = (length + UNIT - 1) // UNIT

    @pl.when(index == 0)
    def prepare():
        for n, cache_ref in enumerate(cache_refs):
            at = pl.ds(pl.multiple_of(ahead(n, shares, "req") * share, share), share)
            keys[at] = cache_ref[0]
            values[at] = cache_ref[1]
        for n in range(0, shares * share, UNIT):
            at = slice(n, n + UNIT)
            seen = lax.broadcasted_iota(jnp.int32, (UNIT, depth), 0) + n < length
            keys[at] = jnp.where(seen, keys[at], keys[0:1])
            flipped[:depth, at] = jnp.where(seen, values[at].astype(jnp.float32), 0.0).T.astype(jnp.bfloat16)
        column = lax.broadcasted_iota(jnp.int32, (ONES, shares * share), 1)
        flipped[depth:] = jnp.where(column < length, 1.0, 0.0).astype(jnp.bfloat16)

    def score(at, cut):
        return dot(keys[at], q_ref[0, cut], ((1,), (1,))) * factor

    def mix(at, weights):
        return dot(flipped[:, at], weights.astype(jnp.bfloat16), ((1,), (0,)))

    total[...] = state_ref[0]

    def over(at):
        scores = score(at, tiles[0])
        for n, cut in enumerate(tiles):
            later = score(at, tiles[n + 1]) if n + 1 < len(tiles) else None
            total[:, cut] += mix(at, jnp.exp2(scores - top_ref[0, :, cut]))
            scores = later

    def step(pair, carry):
        over(pl.ds(pl.multiple_of(pair * 2 * UNIT, 2 * UNIT), 2 * UNIT))
        return carry

    lax.fori_loop(0, count // 2, step, 0)

    @pl.when(count % 2 == 1)
    def lone():
        over(pl.ds(pl.multiple_of((count - 1) * UNIT, UNIT), UNIT))

    @pl.when(jnp.logical_not(jnp.max(total[depth : depth + 1]) < CEILING))
    def redo():
        small = UNIT

        def column(c, carry):
            cut = pl.ds(pl.multiple_of(c * small, small), small)
            query = q_ref[0, cut]
            token = lax.broadcasted_iota(jnp.int32, (1, small), 1) + c * small + index * block

            def grow(state, scores, values):
                highest, mixed = state
                higher = jnp.maximum(highest, jnp.max(scores, axis=0, keepdims=True))
                weights = jnp.exp2(scores - higher)
                return higher, mixed * jnp.exp2(highest - higher) + values(weights)

            def cached(u, state):
                at = pl.ds(pl.multiple_of(u * UNIT, UNIT), UNIT)
                return grow(state, dot(keys[at], query, ((1,), (1,))) * factor, functools.partial(mix, at))

            def over_new(state, n, new_ref):
                scores = dot(new_ref[0, 0], query, ((1,), (1,))) * factor
                first = ahead(n, fresh, "qh") * new_ref.shape[2]
                key = lax.broadcasted_iota(jnp.int32, scores.shape, 0) + first

                def values(weights):
                    mixed = dot(new_ref[1, 0], weights.astype(jnp.bfloat16), ((0,), (0,)))
                    sums = jnp.sum(weights, axis=0, keepdims=True)
                    return jnp.concatenate([mixed, jnp.broadcast_to(sums, (ONES, small))])

                return grow(state, jnp.where(key <= token // heads, scores, -jnp.inf), values)

            state = (jnp.full((1, small), -1e30, jnp.float32), jnp.zeros((depth + ONES, small), jnp.float32))
            state = lax.fori_loop(0, count, cached, state)
            for n, new_ref in enumerate(new_refs):
                state = over_new(state, n, new_ref)
            total[:, cut] = state[1]
            return carry

        lax.fori_loop(0, block // small, column, 0)

    for cut in tiles:
        out_ref[0, cut] = (total[:depth, cut] / total[depth : depth + 1, cut]).T.astype(jnp.bfloat16)


def attend_cache(heads, request, lengths, queries, cache, new, state, top, after):
    _, rows, depth = queries.shape
    shares, share = len(cache), cache[0].shape[1]
    block = TOKENS * heads
    part = pl.BlockSpec((1, block, depth), lambda i, _: (request, i, 0))
    return pl.pallas_call(
        functools.partial(cache_kernel, heads, request, shares, len(new)),
        grid_spec=pltpu.PrefetchScalarGridSpec(
            num_scalar_prefetch=1,
            grid=(rows // block,),
            in_specs=[
                part,
                pl.BlockSpec((1, depth + ONES, block), lambda i, _: (0, 0, i)),
                pl.BlockSpec((1, 1, block), lambda i, _: (0, 0, i)),
                *[pl.BlockSpec((2, share, depth), lambda i, _: (0, 0, 0))] * shares,
                *[pl.BlockSpec((2, 1, n.shape[2], depth), lambda i, _: (0, request, 0, 0)) for n in new],
                pl.BlockSpec(memory_space=pl.ANY),
            ],
            out_specs=part,
            scratch_shapes=[
                pltpu.VMEM((shares * share, depth), jnp.bfloat16),
                pltpu.VMEM((shares * share, depth), jnp.bfloat16),
                pltpu.VMEM((depth + ONES, shares * share), jnp.bfloat16),
                pltpu.VMEM((depth + ONES, block), jnp.float32),
            ],
        ),
        out_shape=jax.ShapeDtypeStruct(queries.shape, jnp.bfloat16),
        input_output_aliases={4 + shares + len(new): 0} if after.shape == queries.shape else {},
        compiler_params=pltpu.CompilerParams(vmem_limit_bytes=30 << 20),
        name="attend_cache",
    )(lengths, queries, state, top, *cache, *new, after)


def on_device(queries, stretch_keys, stretch_values, cache_keys, cache_values, slot_of_req, cache_len):
    local, stretch, head_count, depth = queries.shape
    flat = queries.reshape(local, stretch * head_count, depth)
    blocks = share_slots(cache_keys, cache_values, head_count)
    spread = send_back(blocks, "req")
    new = send_back(split_stretch(stretch_keys, stretch_values, head_count, blocks[0]), "qh")
    states = [attend_stretch(head_count, 0, flat, new, blocks[0])]
    ordered = order_shares(spread, slot_of_req, states[0][1])
    caches = [send_back(ordered[n], "req") for n in range(local)]
    for n in range(1, local):
        states.append(attend_stretch(head_count, n, flat, new, ordered[-1][0]))
    out = states[-1][1]
    for n in range(local):
        out = attend_cache(head_count, n, cache_len, flat, caches[n], new, *states[n], out)
    return out.reshape(queries.shape)


def solution(mesh):
    return jax.shard_map(
        on_device,
        mesh=mesh,
        in_specs=(
            P("req", None, ("kvh", "qh"), None),
            P("req", "qh", "kvh", None),
            P("req", "qh", "kvh", None),
            P("req", None, "kvh", None),
            P("req", None, "kvh", None),
            P(),
            P("req"),
        ),
        out_specs=P("req", None, ("kvh", "qh"), None),
        check_vma=False,
    )
```
